512 devices in a mesh: nodes: 256 (over z, y, x), heads: 2 (over core).
Axes of the slice: x: 4, y: 8, z: 8, core: 2. Of those that a mesh axis runs over, the one named last changes fastest.
Arguments:
- features: bfloat16 [196608, 512], P(('nodes', 'heads')), may hold values from -24 to 24
- w_qkv: bfloat16 [512, 3, 512], replicated, may hold values from -0.25 to 0.25
- w_out: bfloat16 [512, 512], replicated, may hold values from -0.25 to 0.25
- w_up: bfloat16 [512, 1024], replicated, may hold values from -0.25 to 0.25
- w_down: bfloat16 [1024, 512], replicated, may hold values from -0.1875 to 0.1875
- pattern: int32 [1536, 128, 8], P(('nodes', 'heads')), may hold values from 0 to 65535
- partner: int32 [1536, 4], P(('nodes', 'heads')), may hold values from 0 to 2, as said below
- counts: int32 [512], P(('nodes', 'heads')), may hold values from 1 to 3, as said below
Outputs:
- mixed: bfloat16 [196608, 512], P(('nodes', 'heads'))
The draws below stay inside these ranges and needn't reach their ends.
Inputs may be any that keep to these rules, and one draw needn't show every extreme that they name: `partner`: each link of block slot s of device d names a live block slot of device d XOR 2**b_l; every live slot of that device is named by some slot of d. `counts`: some device holds 3 live blocks.
All inputs are finite; a program needn't handle non-finite values.
Results may differ from the reference program's by a relative error of at most 0.012.
The reference program's roundings to bfloat16 on the way (of `projected`, `weights`, `attended` and `hidden`) count: a program that leaves them out, or rounds other values in their place, can miss the bound.
Values may be sent and summed in bfloat16 or wider, within the bound.
No kernel may reach another device: no remote copies, remote signals or barrier semaphores. Data moves between devices by JAX's collectives and lax.ppermute only.
A program may use at most 64 MiB of HBM per device.

```python
import jax
import jax.numpy as jnp
from jax import lax

D = 512
H = 8
FF = 1024
BLK = 128
SLOTS = 3
NBLKS = 1536
NODES = 196608
DEVICES = 512


def live_counts(key):
    base = jax.random.randint(jax.random.fold_in(key, 101), (DEVICES,), max(1, SLOTS // 3), SLOTS + 1)
    fullest = jax.random.randint(jax.random.fold_in(key, 102), (), 0, DEVICES)
    return jnp.where(jnp.arange(DEVICES) == fullest, SLOTS, base).astype(jnp.int32)


def draw_counts(key, part):
    return live_counts(key)


def draw_partner(key, part):
    live = live_counts(key)
    key = jax.random.fold_in(key, 7)
    log_size = DEVICES.bit_length() - 1
    device = jnp.arange(DEVICES).astype(jnp.int32)
    columns = []
    for link_index in range(4):
        linked_dev = jnp.bitwise_xor(device, 1 << link_index * log_size // 4)
        row_keys = jax.random.split(jax.random.fold_in(key, link_index), DEVICES)
        orders = jax.vmap(lambda one_key: jax.random.permutation(one_key, SLOTS))(row_keys).astype(jnp.int32)
        columns.append(orders % live[linked_dev][:, None])
    return jnp.stack(columns, axis=-1).reshape(NBLKS, 4).astype(jnp.int32)


def draw_features(key, part):
    key = jax.random.fold_in(key, 11)
    position = jnp.arange(D).astype(jnp.float32) / (D - 1)
    column_factor = 0.6 + 0.8 * jax.random.uniform(jax.random.fold_in(key, 1), (D,), jnp.float32)
    base = jnp.clip(jax.random.normal(jax.random.fold_in(key, 2), (NODES, D), jnp.float32), -4.0, 4.0)
    rise = 3.0 ** position
    return (base * rise * column_factor).astype(jnp.bfloat16)


def touch_ends(array, rng, low, top_value):
    index_at = [jax.random.randint(jax.random.fold_in(rng, axis), (), 0, length) for axis, length in enumerate(array.shape)]
    widest = array.shape.index(max(array.shape))
    beside = index_at[:widest] + [(index_at[widest] + 1) % array.shape[widest]] + index_at[widest + 1:]
    return array.at[tuple(index_at)].set(low).at[tuple(beside)].set(top_value)


def bell_draw(stream_key, dims, scale, bound, kind=jnp.bfloat16):
    array = scale * jax.random.normal(stream_key, dims, jnp.float32)
    return jnp.clip(array, min=-bound, max=bound).astype(kind)


def setup_inputs(seed: int = 0) -> dict:
    key_of = jax.random.split(jax.random.key(seed), 9)
    features = draw_features(jax.random.fold_in(key_of[8], 71), 0)
    w_qkv = bell_draw(key_of[1], (D, 3, D), D ** -0.5, 0.25)
    w_out = bell_draw(key_of[2], (D, D), D ** -0.5, 0.25)
    w_up = bell_draw(key_of[3], (D, FF), D ** -0.5, 0.25)
    w_down = bell_draw(key_of[4], (FF, D), FF ** -0.5, 0.1875)
    pattern = touch_ends(jax.random.randint(key_of[5], (NBLKS, BLK, BLK // 16), 0, 65536), jax.random.fold_in(key_of[5], 1), 0, 65535).astype(jnp.int32)
    partner = draw_partner(jax.random.fold_in(key_of[8], 71), 0)
    counts = draw_counts(jax.random.fold_in(key_of[8], 71), 0)
    return dict(features=features, w_qkv=w_qkv, w_out=w_out, w_up=w_up, w_down=w_down, pattern=pattern, partner=partner, counts=counts)


epsilon = 1e-05

def unpack_bits(pattern_words, width):
    column = jnp.arange(width).astype(jnp.int32)
    picked = pattern_words[..., column // 16]
    bits = jnp.right_shift(picked, column % 16) & 1
    return (bits == 1) | jnp.eye(width, dtype=bool)

def reference(features, w_qkv, w_out, w_up, w_down, pattern, partner, counts):
    head_size = D // H
    projected = jnp.dot(features, w_qkv.reshape(D, 3 * D), preferred_element_type=jnp.float32)
    projected = projected.reshape(NODES, 3, D).astype(jnp.bfloat16)
    blocks = projected.reshape(NBLKS, BLK, 3, D)
    log_size = DEVICES.bit_length() - 1
    block_ids = jnp.arange(NBLKS).astype(jnp.int32)
    device = block_ids // SLOTS
    linked = jnp.stack([jnp.bitwise_xor(device, 1 << link_index * log_size // 4) * SLOTS + partner[:, link_index] for link_index in range(4)], axis=1).astype(jnp.int32)
    allowed_local = unpack_bits(pattern, BLK)
    score_scale = 1.0 / head_size ** 0.5

    def attend(item):
        index, others, local = item
        own = blocks[index]
        far = blocks[others]
        keys_values = jnp.concatenate([own[None, :, 1:], far[:, :, 1:]], axis=0).reshape(5 * BLK, 2, D)
        queries = own[:, 0].reshape(BLK, H, head_size).astype(jnp.float32)
        keys = keys_values[:, 0].reshape(5 * BLK, H, head_size).astype(jnp.float32)
        values = keys_values[:, 1].reshape(5 * BLK, H, head_size).astype(jnp.float32)
        scores = jnp.einsum('qhe,khe->hqk', queries, keys) * score_scale
        allowed = jnp.concatenate([local, jnp.ones((BLK, 4 * BLK), dtype=bool)], axis=1)
        scores = jnp.where(allowed[None], scores, -1e+30)
        top_score = lax.optimization_barrier(jnp.max(scores, axis=-1, keepdims=True))
        expo = jnp.exp(scores - top_score)
        weights = (expo / lax.optimization_barrier(jnp.sum(expo, axis=-1, keepdims=True))).astype(jnp.bfloat16)
        result = jnp.einsum('hqk,khe->qhe', weights.astype(jnp.float32), values)
        return result.astype(jnp.bfloat16).reshape(BLK, D)
    attended = lax.map(attend, (block_ids, linked, allowed_local)).reshape(NODES, D)
    resid = features.astype(jnp.float32) + jnp.dot(attended, w_out, preferred_element_type=jnp.float32)
    row_mean = lax.optimization_barrier(jnp.mean(resid, axis=1, keepdims=True))
    row_var = lax.optimization_barrier(jnp.mean(resid * resid, axis=1, keepdims=True)) - row_mean * row_mean
    normed = (resid - row_mean) * lax.rsqrt(row_var + epsilon)
    hidden = jax.nn.relu(jnp.dot(normed.astype(jnp.bfloat16), w_up, preferred_element_type=jnp.float32)).astype(jnp.bfloat16)
    ffn = jnp.dot(hidden, w_down, preferred_element_type=jnp.float32)
    mixed = normed + ffn
    live = block_ids % SLOTS < counts[device]
    live_rows = jnp.repeat(live, BLK)
    return jnp.where(live_rows[:, None], mixed, 0.0).astype(jnp.bfloat16)
```

```python
import jax
import jax.numpy as jnp
from jax import lax
from jax.experimental import pallas as pl
from jax.experimental.pallas import tpu as pltpu
from jax.sharding import PartitionSpec as P

D = 512
H = 8
HEAD = D // H
BLK = 128
SLOTS = 3
ROWS = SLOTS * BLK
PAIRS = H // 2
EPSILON = 1e-05
SCALE = 1.4426950408889634 / HEAD**0.5
F32 = jnp.float32
BF16 = jnp.bfloat16


def from_partner(value, axis, bit):
    mask = 2**bit
    pairs = [(source, source ^ mask) for source in range(lax.axis_size(axis))]
    return lax.ppermute(value, axis, pairs)


def mm(a, b):
    return jnp.dot(a, b, preferred_element_type=F32)


def low_half(shape):
    return lax.broadcasted_iota(jnp.int32, shape, 1) < HEAD


def split_heads(pair):
    low = low_half(pair.shape)
    zero = jnp.zeros_like(pair)
    return jnp.where(low, pair, zero), jnp.where(low, zero, pair)


def attend(q, k, v, allowed):
    q_low, q_high = split_heads(q)
    scores = lax.dot_general(
        jnp.concatenate([q_low, q_high], axis=0), k, (((1,), (1,)), ((), ())), preferred_element_type=F32
    )
    if allowed is not None:
        scores = jnp.where(allowed, scores, -1e30)
    top = jnp.max(scores, axis=1, keepdims=True)
    weights = jnp.exp2((scores - top) * SCALE).astype(BF16)
    weights = jnp.concatenate([weights[:BLK], weights[BLK:]], axis=1)
    v_low, v_high = split_heads(v)
    one_low, one_high = split_heads(jnp.ones_like(v))
    values = jnp.concatenate(
        [jnp.concatenate([v_low, one_low], axis=1), jnp.concatenate([v_high, one_high], axis=1)], axis=0
    )
    result = mm(weights, values)
    low = low_half((BLK, 2 * HEAD))
    return result[:, : 2 * HEAD], result[:, 2 * HEAD :], jnp.where(low, top[:BLK], top[BLK:])


def merge(first, second):
    o1, l1, m1 = first
    o2, l2, m2 = second
    m = jnp.maximum(m1, m2)
    a = jnp.exp2((m1 - m) * SCALE)
    b = jnp.exp2((m2 - m) * SCALE)
    return o1 * a + o2 * b, l1 * a + l2 * b, m


def local_mask(words):
    word_count = words.shape[0]
    halves = jnp.concatenate([words & 255, jnp.right_shift(words, 8)], axis=0).astype(F32).astype(BF16)
    row = lax.broadcasted_iota(jnp.int32, (2 * word_count, BLK), 0)
    column = lax.broadcasted_iota(jnp.int32, (2 * word_count, BLK), 1)
    source = column // 16 + word_count * (column % 16 // 8)
    pick = jnp.where(row == source, 1.0, 0.0).astype(BF16)
    picked = lax.dot_general(halves, pick, (((0,), (0,)), ((), ())), preferred_element_type=F32)
    query = lax.broadcasted_iota(jnp.int32, (BLK, BLK), 0)
    key = lax.broadcasted_iota(jnp.int32, (BLK, BLK), 1)
    bits = jnp.right_shift(picked.astype(jnp.int32), key % 8) & 1
    return (bits == 1) | (query == key)


def slot_rows(slot):
    return pl.ds(pl.multiple_of(slot * BLK, BLK), BLK)


def pair_columns(pair):
    return slice(pair * 2 * HEAD, (pair + 1) * 2 * HEAD)


def own_kernel(link, partner, x, r, w, words, q_out, o_out, l_out, m_out, k_own, v_own, k_far, v_far):
    q_out[...] = mm(x[...], w[0]).astype(BF16)
    k_own[...] = mm(x[...], w[1]).astype(BF16)
    v_own[...] = mm(x[...], w[2]).astype(BF16)
    k_far[...] = mm(r[...], w[1]).astype(BF16)
    v_far[...] = mm(r[...], w[2]).astype(BF16)
    for s in range(SLOTS):
        rows = slice(s * BLK, (s + 1) * BLK)
        far = slot_rows(partner[s, link])
        mask = local_mask(words[s])
        mask = jnp.concatenate([mask, jnp.ones((BLK, BLK), dtype=jnp.bool_)], axis=1)
        mask = jnp.concatenate([mask, mask], axis=0)
        for p in range(PAIRS):
            cols = pair_columns(p)
            k = jnp.concatenate([k_own[rows, cols], k_far[far, cols]], axis=0)
            v = jnp.concatenate([v_own[rows, cols], v_far[far, cols]], axis=0)
            o, l, m = attend(q_out[rows, cols], k, v, mask)
            o_out[rows, cols] = o
            l_out[rows, cols] = l
            m_out[rows, cols] = m


def far_kernel(link_a, link_b, partner, ra, rb, w, q, o_in, l_in, m_in, o_out, l_out, m_out, ka, va, kb, vb):
    ka[...] = mm(ra[...], w[1]).astype(BF16)
    va[...] = mm(ra[...], w[2]).astype(BF16)
    kb[...] = mm(rb[...], w[1]).astype(BF16)
    vb[...] = mm(rb[...], w[2]).astype(BF16)
    for s in range(SLOTS):
        rows = slice(s * BLK, (s + 1) * BLK)
        far_a = slot_rows(partner[s, link_a])
        far_b = slot_rows(partner[s, link_b])
        for p in range(PAIRS):
            cols = pair_columns(p)
            k = jnp.concatenate([ka[far_a, cols], kb[far_b, cols]], axis=0)
            v = jnp.concatenate([va[far_a, cols], vb[far_b, cols]], axis=0)
            part = attend(q[rows, cols], k, v, None)
            o, l, m = merge((o_in[rows, cols], l_in[rows, cols], m_in[rows, cols]), part)
            o_out[rows, cols] = o
            l_out[rows, cols] = l
            m_out[rows, cols] = m


def last_kernel(link, partner, counts, r, w, q, o_in, l_in, m_in, x, w_out, w_up, w_down, out, k_far, v_far, att):
    k_far[...] = mm(r[...], w[1]).astype(BF16)
    v_far[...] = mm(r[...], w[2]).astype(BF16)
    for s in range(SLOTS):
        rows = slice(s * BLK, (s + 1) * BLK)
        far = slot_rows(partner[s, link])
        for p in range(PAIRS):
            cols = pair_columns(p)
            part = attend(q[rows, cols], k_far[far, cols], v_far[far, cols], None)
            o, l, _ = merge((o_in[rows, cols], l_in[rows, cols], m_in[rows, cols]), part)
            att[rows, cols] = (o / l).astype(BF16)
    resid = x[...].astype(F32) + mm(att[...], w_out[...])
    mean = jnp.mean(resid, axis=1, keepdims=True)
    var = jnp.mean(resid * resid, axis=1, keepdims=True) - mean * mean
    normed = (resid - mean) * lax.rsqrt(var + EPSILON)
    hidden = jnp.maximum(mm(normed.astype(BF16), w_up[...]), 0.0).astype(BF16)
    mixed = normed + mm(hidden, w_down[...])
    slot = lax.broadcasted_iota(jnp.int32, (ROWS, 1), 0) // BLK
    out[...] = jnp.where(slot < counts[0], mixed, 0.0).astype(BF16)


VMEM = pl.BlockSpec(memory_space=pltpu.VMEM)
SMEM = pl.BlockSpec(memory_space=pltpu.SMEM)


def wide(dtype):
    return jax.ShapeDtypeStruct((ROWS, D), dtype)


def scratch(n):
    return [pltpu.VMEM((ROWS, D), BF16) for _ in range(n)]


def call(kernel, smem, vmem, outs, n_scratch, flops, name):
    return pl.pallas_call(
        kernel,
        out_shape=outs,
        in_specs=[SMEM] * len(smem) + [VMEM] * len(vmem),
        out_specs=jax.tree.map(lambda _: VMEM, outs),
        scratch_shapes=scratch(n_scratch),
        compiler_params=pltpu.CompilerParams(vmem_limit_bytes=24 * 2**20),
        cost_estimate=pl.CostEstimate(flops=flops, bytes_accessed=4 * 2**20, transcendentals=0),
        name=name,
    )(*smem, *vmem)


def local(features, w_qkv, w_out, w_up, w_down, pattern, partner, counts):
    log_size = (lax.axis_size("nodes") * lax.axis_size("heads")).bit_length() - 1
    bits = [link * log_size // 4 for link in range(4)]
    received = {}
    for link in (2, 1, 3, 0):
        bit = bits[link]
        received[link] = (
            from_partner(features, "heads", 0) if bit == 0 else from_partner(features, "nodes", bit - 1)
        )
    w = jnp.transpose(w_qkv, (1, 0, 2))
    words = jnp.transpose(pattern, (0, 2, 1))
    state = [wide(F32)] * 3
    q, *parts = call(
        lambda *refs: own_kernel(0, *refs),
        [partner], [features, received[0], w, words], [wide(BF16)] + state, 4, 2 * 10**9, "own_and_core",
    )
    parts = call(
        lambda *refs: far_kernel(1, 3, *refs),
        [partner], [received[1], received[3], w, q, *parts], state, 4, 2 * 10**9, "far_x_z",
    )
    return call(
        lambda *refs: last_kernel(2, *refs),
        [partner, counts], [received[2], w, q, *parts, features, w_out, w_up, w_down], wide(BF16), 3, 2 * 10**9, "far_y_mix",
    )


def solution(mesh):
    placed = (
        P(("nodes", "heads"), None),
        P(),
        P(),
        P(),
        P(),
        P(("nodes", "heads"), None, None),
        P(("nodes", "heads"), None),
        P(("nodes", "heads")),
    )
    return jax.shard_map(
        local, mesh=mesh, in_specs=placed, out_specs=P(("nodes", "heads"), None), check_vma=False
    )
```

```python
import jax
import jax.numpy as jnp
from jax import lax
from jax.experimental import pallas as pl
from jax.experimental.pallas import tpu as pltpu
from jax.sharding import PartitionSpec as P

D = 512
H = 8
HEAD = D // H
BLK = 128
SLOTS = 3
ROWS = SLOTS * BLK
PAIRS = H // 2
EPSILON = 1e-05
SCALE = 1.4426950408889634 / HEAD**0.5
F32 = jnp.float32
BF16 = jnp.bfloat16


def from_partner(value, axis, bit):
    mask = 2**bit
    pairs = [(source, source ^ mask) for source in range(lax.axis_size(axis))]
    return lax.ppermute(value, axis, pairs)


def mm(a, b):
    return jnp.dot(a, b, preferred_element_type=F32)


def mm_nt(a, b):
    return lax.dot_general(a, b, (((1,), (1,)), ((), ())), preferred_element_type=F32)


def block(index):
    return slice(index * BLK, (index + 1) * BLK)


def head_rows(head):
    return slice(head * HEAD, (head + 1) * HEAD)


def local_mask(words):
    word_count = words.shape[0]
    halves = jnp.concatenate([words & 255, jnp.right_shift(words, 8)], axis=0).astype(F32).astype(BF16)
    key = lax.broadcasted_iota(jnp.int32, (BLK, 2 * word_count), 0)
    row = lax.broadcasted_iota(jnp.int32, (BLK, 2 * word_count), 1)
    source = key // 16 + word_count * (key % 16 // 8)
    pick = jnp.where(row == source, 1.0, 0.0).astype(BF16)
    picked = mm(pick, halves)
    key = lax.broadcasted_iota(jnp.int32, (BLK, BLK), 0)
    query = lax.broadcasted_iota(jnp.int32, (BLK, BLK), 1)
    bits = jnp.right_shift(picked.astype(jnp.int32), key % 8) & 1
    return (bits == 1) | (query == key)


def spread(q_pair):
    low = lax.broadcasted_iota(jnp.int32, q_pair.shape, 0) < HEAD
    zero = jnp.zeros_like(q_pair)
    return jnp.concatenate([jnp.where(low, q_pair, zero), jnp.where(low, zero, q_pair)], axis=1)


def attend(q_spread, keys, values, allowed):
    scores = jnp.concatenate([mm(keys(p), q_spread(p)) for p in range(PAIRS)], axis=1)
    if allowed is not None:
        scores = jnp.where(jnp.concatenate([allowed] * H, axis=1), scores, -1e30)
    top = jnp.max(scores, axis=0, keepdims=True)
    expo = jnp.exp2((scores - top) * SCALE)
    total = jnp.sum(expo, axis=0, keepdims=True)
    weights = expo.astype(BF16)
    return top, total, [mm(values[head_rows(h)], weights[:, block(h)]) for h in range(H)]


def project(x, wk, wvt, k_held, v_held):
    k_held[...] = mm(x, wk).astype(BF16)
    values = mm_nt(wvt, x).astype(BF16)
    for s in range(SLOTS):
        v_held[s] = values[:, block(s)]


def own_kernel(x_in, w, words, x_out, qs_out, wk_out, wvt_out, o_out, m_out, l_out, k_held, v_held):
    x = x_in.at[pl.ds(0, ROWS)]
    x_out[...] = x[...]
    wk_out[...] = w[1]
    wvt_out[...] = w[2].T
    project(x[...], wk_out[...], wvt_out[...], k_held, v_held)
    q = mm(x[...], w[0]).astype(BF16).T
    for s in range(SLOTS):
        for p in range(PAIRS):
            qs_out[s, p] = spread(q[block(p), block(s)])
        top, total, parts = attend(
            lambda p: qs_out[s, p], lambda p: k_held[block(s), block(p)], v_held[s], local_mask(words[s])
        )
        m_out[s] = top
        l_out[s] = total
        for h in range(H):
            o_out[head_rows(h), block(s)] = parts[h]


def merged(s, link, partner, qs, o_in, m_in, l_in, k_held, v_held):
    slot = partner[s, link]
    rows = pl.ds(pl.multiple_of(slot * BLK, BLK), BLK)
    top, total, parts = attend(lambda p: qs[s, p], lambda p: k_held[rows, block(p)], v_held[slot], None)
    m = jnp.maximum(m_in[s], top)
    old = jnp.exp2((m_in[s] - m) * SCALE)
    new = jnp.exp2((top - m) * SCALE)
    both = [
        o_in[head_rows(h), block(s)] * old[:, block(h)] + parts[h] * new[:, block(h)] for h in range(H)
    ]
    return m, l_in[s] * old + total * new, both


def far_kernel(link, partner_hbm, wk, wvt, qs, o_in, m_in, l_in, x, o_out, m_out, l_out, partner, k_held, v_held, sems):
    copy = pltpu.make_async_copy(partner_hbm, partner, sems.at[0])
    copy.start()
    if link == 0:
        other = pl.ds(pl.multiple_of((1 - lax.axis_index("heads")) * ROWS, ROWS), ROWS)
        x = x.at[other]
    project(x[...], wk[...], wvt[...], k_held, v_held)
    copy.wait()
    for s in range(SLOTS):
        m, l, both = merged(s, link, partner, qs, o_in, m_in, l_in, k_held, v_held)
        m_out[s] = m
        l_out[s] = l
        for h in range(H):
            o_out[head_rows(h), block(s)] = both[h]


def last_kernel(
    link, partner_hbm, counts_hbm, wk, wvt, qs, o_in, m_in, l_in, x, w_out, w_up, w_down, r, out,
    partner, counts, k_held, v_held, att, sems,
):
    copies = [
        pltpu.make_async_copy(partner_hbm, partner, sems.at[0]),
        pltpu.make_async_copy(counts_hbm, counts, sems.at[1]),
    ]
    for copy in copies:
        copy.start()
    project(r[pl.ds(0, ROWS)], wk[...], wvt[...], k_held, v_held)
    for copy in copies:
        copy.wait()
    for s in range(SLOTS):
        _, l, both = merged(s, link, partner, qs, o_in, m_in, l_in, k_held, v_held)
        share = 1.0 / l
        for p in range(PAIRS):
            pair = [both[h] * share[:, block(h)] for h in (2 * p, 2 * p + 1)]
            att[block(s), block(p)] = jnp.concatenate(pair, axis=0).astype(BF16).T
    resid = x[...].astype(F32) + mm(att[...], w_out[...])
    mean = jnp.mean(resid, axis=1, keepdims=True)
    var = jnp.mean(resid * resid, axis=1, keepdims=True) - mean * mean
    normed = (resid - mean) * lax.rsqrt(var + EPSILON)
    hidden = jnp.maximum(mm(normed.astype(BF16), w_up[...]), 0.0).astype(BF16)
    mixed = normed + mm(hidden, w_down[...])
    slot = lax.broadcasted_iota(jnp.int32, (ROWS, 1), 0) // BLK
    out[...] = jnp.where(slot < counts[0], mixed, 0.0).astype(BF16)


VMEM = pl.BlockSpec(memory_space=pltpu.VMEM)
ANY = pl.BlockSpec(memory_space=pltpu.HBM)
SPREAD = jax.ShapeDtypeStruct((SLOTS, PAIRS, BLK, 2 * BLK), BF16)
WEIGHT = jax.ShapeDtypeStruct((D, D), BF16)
STATE = (
    jax.ShapeDtypeStruct((D, ROWS), F32),
    jax.ShapeDtypeStruct((SLOTS, 1, H * BLK), F32),
    jax.ShapeDtypeStruct((SLOTS, 1, H * BLK), F32),
)
HELD = [pltpu.VMEM((ROWS, D), BF16), pltpu.VMEM((SLOTS, D, BLK), BF16)]
PARTNER = pltpu.SMEM((SLOTS, 4), jnp.int32)


PAD = 400


def stage_kernel(x, x_out):
    x_out[pl.ds(0, ROWS)] = x[...]


def stage(x):
    return pl.pallas_call(
        stage_kernel,
        out_shape=jax.ShapeDtypeStruct((PAD, D), BF16),
        in_specs=[VMEM],
        out_specs=VMEM,
        compiler_params=pltpu.CompilerParams(vmem_limit_bytes=4 * 2**20),
        cost_estimate=pl.CostEstimate(flops=0, bytes_accessed=8 * 2**20, transcendentals=0),
        name="stage",
    )(x)


def call(kernel, outside, inside, outs, scratch, name):
    return pl.pallas_call(
        kernel,
        out_shape=outs,
        in_specs=[ANY] * len(outside) + [VMEM] * len(inside),
        out_specs=jax.tree.map(lambda _: VMEM, outs),
        scratch_shapes=scratch,
        compiler_params=pltpu.CompilerParams(vmem_limit_bytes=12 * 2**20),
        cost_estimate=pl.CostEstimate(flops=0, bytes_accessed=0, transcendentals=0),
        name=name,
    )(*outside, *inside)


def local(features, w_qkv, w_out, w_up, w_down, pattern, partner, counts):
    log_size = (lax.axis_size("nodes") * lax.axis_size("heads")).bit_length() - 1
    bits = [link * log_size // 4 for link in range(4)]

    def exchange(value, link):
        bit = bits[link]
        return from_partner(value, "heads", 0) if bit == 0 else from_partner(value, "nodes", bit - 1)

    w = jnp.transpose(w_qkv, (1, 0, 2))
    words = jnp.transpose(pattern, (0, 2, 1))
    here = lax.axis_index("nodes") < lax.axis_size("nodes")

    def own(x):
        return call(
            own_kernel, [], [x, w, words], (jax.ShapeDtypeStruct((ROWS, D), BF16), SPREAD, WEIGHT, WEIGHT, *STATE),
            HELD, "own",
        )

    def far(link, x, fixed, state):
        return call(
            lambda *refs: far_kernel(link, *refs), [partner], [*fixed, *state, x], STATE,
            [PARTNER, *HELD, pltpu.SemaphoreType.DMA((1,))], "far",
        )

    def zeros(shapes):
        return tuple(jnp.zeros(shape.shape, shape.dtype) for shape in shapes)

    x = stage(features)
    received = {2: exchange(x, 2)}
    for link in (1, 3):
        received[link] = exchange(features, link)
    again, qs, wk, wvt, *state = own(x)
    fixed = (wk, wvt, qs)
    received[0] = lax.all_gather(again, "heads").reshape(2 * ROWS, D)
    for link in (0, 1, 3):
        state = far(link, received[link], fixed, state)
    parts = (*fixed, *state)
    received = received[2]
    return call(
        lambda *refs: last_kernel(2, *refs), [partner, counts], [*parts, again, w_out, w_up, w_down, received],
        jax.ShapeDtypeStruct((ROWS, D), BF16),
        [PARTNER, pltpu.SMEM((1,), jnp.int32), *HELD, pltpu.VMEM((ROWS, D), BF16), pltpu.SemaphoreType.DMA((2,))], "last",
    )


def solution(mesh):
    placed = (
        P(("nodes", "heads"), None),
        P(),
        P(),
        P(),
        P(),
        P(("nodes", "heads"), None, None),
        P(("nodes", "heads"), None),
        P(("nodes", "heads")),
    )
    return jax.shard_map(
        local, mesh=mesh, in_specs=placed, out_specs=P(("nodes", "heads"), None), check_vma=False
    )
```

```python
import jax
import jax.numpy as jnp
from jax import lax
from jax.experimental import pallas as pl
from jax.experimental.pallas import tpu as pltpu
from jax.sharding import PartitionSpec as P

D = 512
H = 8
HEAD = D // H
BLK = 128
SLOTS = 3
ROWS = SLOTS * BLK
PAIRS = H // 2
EPSILON = 1e-05
SCALE = 1.4426950408889634 / HEAD**0.5
F32 = jnp.float32
BF16 = jnp.bfloat16


def from_partner(value, axis, bit):
    mask = 2**bit
    pairs = [(source, source ^ mask) for source in range(lax.axis_size(axis))]
    return lax.ppermute(value, axis, pairs)


def mm(a, b):
    return jnp.dot(a, b, preferred_element_type=F32)


def mm_nt(a, b):
    return lax.dot_general(a, b, (((1,), (1,)), ((), ())), preferred_element_type=F32)


def block(index):
    return slice(index * BLK, (index + 1) * BLK)


def head_rows(head):
    return slice(head * HEAD, (head + 1) * HEAD)


def local_mask(words):
    word_count = words.shape[0]
    halves = jnp.concatenate([words & 255, jnp.right_shift(words, 8)], axis=0).astype(F32).astype(BF16)
    key = lax.broadcasted_iota(jnp.int32, (BLK, 2 * word_count), 0)
    row = lax.broadcasted_iota(jnp.int32, (BLK, 2 * word_count), 1)
    source = key // 16 + word_count * (key % 16 // 8)
    pick = jnp.where(row == source, 1.0, 0.0).astype(BF16)
    picked = mm(pick, halves)
    key = lax.broadcasted_iota(jnp.int32, (BLK, BLK), 0)
    query = lax.broadcasted_iota(jnp.int32, (BLK, BLK), 1)
    bits = jnp.right_shift(picked.astype(jnp.int32), key % 8) & 1
    return (bits == 1) | (query == key)


def spread(q_pair):
    low = lax.broadcasted_iota(jnp.int32, q_pair.shape, 0) < HEAD
    zero = jnp.zeros_like(q_pair)
    return jnp.concatenate([jnp.where(low, q_pair, zero), jnp.where(low, zero, q_pair)], axis=1)


def attend(q_spread, sources):
    scores = []
    for keys, _, allowed in sources:
        score = jnp.concatenate([mm(keys(p), q_spread(p)) for p in range(PAIRS)], axis=1)
        if allowed is not None:
            score = jnp.where(jnp.concatenate([allowed] * H, axis=1), score, -1e30)
        scores.append(score)
    scores = jnp.concatenate(scores, axis=0)
    values = jnp.concatenate([values for _, values, _ in sources], axis=1)
    top = jnp.max(scores, axis=0, keepdims=True)
    expo = jnp.exp2((scores - top) * SCALE)
    total = jnp.sum(expo, axis=0, keepdims=True)
    weights = expo.astype(BF16)
    return top, total, [mm(values[head_rows(h)], weights[:, block(h)]) for h in range(H)]


def project(x, wk, wvt, k_held, v_held):
    k_held[...] = mm(x, wk).astype(BF16)
    values = mm_nt(wvt, x).astype(BF16)
    for s in range(x.shape[0] // BLK):
        v_held[s] = values[:, block(s)]


def named_slot(partner, s, link):
    row = lax.broadcasted_iota(jnp.int32, partner.shape, 0)
    column = lax.broadcasted_iota(jnp.int32, partner.shape, 1)
    return jnp.max(jnp.where((row == s) & (column == link), partner[...].astype(F32), 0.0)).astype(jnp.int32)


def far_source(slot, k_held, v_held):
    rows = pl.ds(pl.multiple_of(slot * BLK, BLK), BLK)
    return lambda p: k_held[rows, block(p)], v_held[slot], None


def own_kernel(partner, both, w, words, qs_out, wk_out, wvt_out, o_out, m_out, l_out, k_held, v_held):
    core = lax.axis_index("heads")
    wk_out[...] = w[1]
    wvt_out[...] = w[2].T
    project(both[...], wk_out[...], wvt_out[...], k_held, v_held)
    q = mm(both[pl.ds(pl.multiple_of(core * ROWS, ROWS), ROWS)], w[0]).astype(BF16).T
    for s in range(SLOTS):
        for p in range(PAIRS):
            qs_out[s, p] = spread(q[block(p), block(s)])
        own_keys, own_values, _ = far_source(core * SLOTS + s, k_held, v_held)
        beside = far_source((1 - core) * SLOTS + named_slot(partner, s, 0), k_held, v_held)
        top, total, parts = attend(lambda p: qs_out[s, p], [(own_keys, own_values, local_mask(words[s])), beside])
        m_out[s] = top
        l_out[s] = total
        for h in range(H):
            o_out[head_rows(h), block(s)] = parts[h]


def pair_block(pair):
    return slice(2 * pair * BLK, 2 * (pair + 1) * BLK)


def merged(s, p, keys, values, qs, o_in, m_in, l_in):
    scores = mm(keys(p), qs[s, p])
    top = jnp.max(scores, axis=0, keepdims=True)
    m_old = m_in[s, :, pair_block(p)]
    m = jnp.maximum(m_old, top)
    old = jnp.exp2((m_old - m) * SCALE)
    expo = jnp.exp2((scores - m) * SCALE)
    l = l_in[s, :, pair_block(p)] * old + jnp.sum(expo, axis=0, keepdims=True)
    weights = expo.astype(BF16)
    o = [
        o_in[head_rows(2 * p + i), block(s)] * old[:, block(i)] + mm(values[head_rows(2 * p + i)], weights[:, block(i)])
        for i in range(2)
    ]
    return m, l, o


def far_kernel(link, partner, wk, wvt, qs, o_in, m_in, l_in, x, o_out, m_out, l_out, k_held, v_held):
    project(x[...], wk[...], wvt[...], k_held, v_held)
    for s in range(SLOTS):
        keys, values, _ = far_source(named_slot(partner, s, link), k_held, v_held)
        for p in range(PAIRS):
            m, l, o = merged(s, p, keys, values, qs, o_in, m_in, l_in)
            m_out[s, :, pair_block(p)] = m
            l_out[s, :, pair_block(p)] = l
            for i in range(2):
                o_out[head_rows(2 * p + i), block(s)] = o[i]


def last_kernel(
    link, partner, counts, wk, wvt, qs, o_in, m_in, l_in, both_x, w_out, w_up, w_down, r, out, k_held, v_held, att, done, sems,
):
    core = lax.axis_index("heads")
    project(r[pl.ds(0, ROWS)], wk[...], wvt[...], k_held, v_held)
    for s in range(SLOTS):
        keys, values, _ = far_source(named_slot(partner, s, link), k_held, v_held)
        for p in range(PAIRS):
            _, l, o = merged(s, p, keys, values, qs, o_in, m_in, l_in)
            share = 1.0 / l
            o = jnp.concatenate([o[i] * share[:, block(i)] for i in range(2)], axis=0)
            att[block(s), block(p)] = o.astype(BF16).T
    x = both_x[pl.ds(pl.multiple_of(core * ROWS, ROWS), ROWS)]
    resid = x.astype(F32) + mm(att[...], w_out[...])
    mean = jnp.mean(resid, axis=1, keepdims=True)
    var = jnp.mean(resid * resid, axis=1, keepdims=True) - mean * mean
    normed = (resid - mean) * lax.rsqrt(var + EPSILON)
    hidden = jnp.maximum(mm(normed.astype(BF16), w_up[...]), 0.0).astype(BF16)
    copies = []
    for s in range(SLOTS):
        mixed = normed[block(s)] + mm(hidden[block(s)], w_down[...])
        done[block(s)] = jnp.where(s < counts[...], mixed, 0.0).astype(BF16)
        copies.append(pltpu.make_async_copy(done.at[block(s)], out.at[block(s)], sems.at[s]))
        copies[s].start()
    for copy in copies:
        copy.wait()


VMEM = pl.BlockSpec(memory_space=pltpu.VMEM)
SMEM = pl.BlockSpec(memory_space=pltpu.SMEM)
SPREAD = jax.ShapeDtypeStruct((SLOTS, PAIRS, BLK, 2 * BLK), BF16)
WEIGHT = jax.ShapeDtypeStruct((D, D), BF16)
STATE = (
    jax.ShapeDtypeStruct((D, ROWS), F32),
    jax.ShapeDtypeStruct((SLOTS, 1, H * BLK), F32),
    jax.ShapeDtypeStruct((SLOTS, 1, H * BLK), F32),
)
HELD = [pltpu.VMEM((ROWS, D), BF16), pltpu.VMEM((SLOTS, D, BLK), BF16)]
BOTH_HELD = [pltpu.VMEM((2 * ROWS, D), BF16), pltpu.VMEM((2 * SLOTS, D, BLK), BF16)]


PAD = 400


def stage_kernel(x, x_out, sems):
    copies = [
        pltpu.make_async_copy(x, x_out.at[pl.ds(0, ROWS)], sems.at[0]),
        pltpu.make_async_copy(x.at[pl.ds(0, PAD - ROWS)], x_out.at[pl.ds(ROWS, PAD - ROWS)], sems.at[1]),
    ]
    for copy in copies:
        copy.start()
    for copy in copies:
        copy.wait()


def stage(x):
    return pl.pallas_call(
        stage_kernel,
        out_shape=jax.ShapeDtypeStruct((PAD, D), BF16),
        in_specs=[pl.BlockSpec(memory_space=pltpu.HBM)],
        out_specs=VMEM,
        scratch_shapes=[pltpu.SemaphoreType.DMA((2,))],
        compiler_params=pltpu.CompilerParams(vmem_limit_bytes=4 * 2**20),
        cost_estimate=pl.CostEstimate(flops=0, bytes_accessed=8 * 2**20, transcendentals=0),
        name="stage",
    )(x)


def call(kernel, scalars, inside, outs, scratch, name, out_space=pltpu.VMEM):
    return pl.pallas_call(
        kernel,
        out_shape=outs,
        in_specs=[VMEM] * (len(scalars) + len(inside)),
        out_specs=jax.tree.map(lambda _: pl.BlockSpec(memory_space=out_space), outs),
        scratch_shapes=scratch,
        compiler_params=pltpu.CompilerParams(vmem_limit_bytes=12 * 2**20),
        cost_estimate=pl.CostEstimate(flops=0, bytes_accessed=0, transcendentals=0),
        name=name,
    )(*scalars, *inside)


def local(features, w_qkv, w_out, w_up, w_down, pattern, partner, counts):
    log_size = (lax.axis_size("nodes") * lax.axis_size("heads")).bit_length() - 1
    bits = [link * log_size // 4 for link in range(4)]

    def exchange(value, link):
        return from_partner(value, "nodes", bits[link] - 1)

    w = jnp.transpose(w_qkv, (1, 0, 2))
    words = jnp.transpose(pattern, (0, 2, 1))
    received = {2: exchange(stage(features), 2)}
    for link in (1, 3):
        received[link] = exchange(features, link)
    both = lax.all_gather(features, "heads").reshape(2 * ROWS, D)
    qs, wk, wvt, *state = call(
        own_kernel, [partner], [both, w, words], (SPREAD, WEIGHT, WEIGHT, *STATE), BOTH_HELD, "own"
    )
    fixed = (wk, wvt, qs)
    for link in (1, 3):
        state = call(
            lambda *refs, link=link: far_kernel(link, *refs), [partner], [*fixed, *state, received[link]], STATE, HELD, "far"
        )
    return call(
        lambda *refs: last_kernel(2, *refs), [partner, counts.reshape(1, 1)],
        [*fixed, *state, both, w_out, w_up, w_down, received[2]],
        jax.ShapeDtypeStruct((ROWS, D), BF16),
        [*HELD, *[pltpu.VMEM((ROWS, D), BF16)] * 2, pltpu.SemaphoreType.DMA((SLOTS,))], "last", pltpu.HBM,
    )


def solution(mesh):
    placed = (
        P(("nodes", "heads"), None),
        P(),
        P(),
        P(),
        P(),
        P(("nodes", "heads"), None, None),
        P(("nodes", "heads"), None),
        P(("nodes", "heads")),
    )
    return jax.shard_map(
        local, mesh=mesh, in_specs=placed, out_specs=P(("nodes", "heads"), None), check_vma=False
    )
```

```python
import jax
import jax.numpy as jnp
from jax import lax
from jax.experimental import pallas as pl
from jax.experimental.pallas import tpu as pltpu
from jax.sharding import PartitionSpec as P

D = 512
H = 8
HEAD = D // H
BLK = 128
SLOTS = 3
ROWS = SLOTS * BLK
PAIRS = H // 2
EPSILON = 1e-05
SCALE = 1.4426950408889634 / HEAD**0.5
F32 = jnp.float32
BF16 = jnp.bfloat16


def from_partner(value, axis, bit):
    mask = 2**bit
    pairs = [(source, source ^ mask) for source in range(lax.axis_size(axis))]
    return lax.ppermute(value, axis, pairs)


def mm(a, b):
    return jnp.dot(a, b, preferred_element_type=F32)


def mm_nt(a, b):
    return lax.dot_general(a, b, (((1,), (1,)), ((), ())), preferred_element_type=F32)


def block(index):
    return slice(index * BLK, (index + 1) * BLK)


def head_rows(head):
    return slice(head * HEAD, (head + 1) * HEAD)


def local_mask(words):
    word_count = words.shape[0]
    halves = jnp.concatenate([words & 255, jnp.right_shift(words, 8)], axis=0).astype(F32).astype(BF16)
    key = lax.broadcasted_iota(jnp.int32, (BLK, 2 * word_count), 0)
    row = lax.broadcasted_iota(jnp.int32, (BLK, 2 * word_count), 1)
    source = key // 16 + word_count * (key % 16 // 8)
    pick = jnp.where(row == source, 1.0, 0.0).astype(BF16)
    picked = mm(pick, halves)
    key = lax.broadcasted_iota(jnp.int32, (BLK, BLK), 0)
    query = lax.broadcasted_iota(jnp.int32, (BLK, BLK), 1)
    bits = jnp.right_shift(picked.astype(jnp.int32), key % 8) & 1
    return (bits == 1) | (query == key)


def spread(q_pair):
    low = lax.broadcasted_iota(jnp.int32, q_pair.shape, 0) < HEAD
    zero = jnp.zeros_like(q_pair)
    return jnp.concatenate([jnp.where(low, q_pair, zero), jnp.where(low, zero, q_pair)], axis=1)


def attend(q_spread, sources):
    scores = []
    for keys, _, allowed in sources:
        score = jnp.concatenate([mm(keys(p), q_spread(p)) for p in range(PAIRS)], axis=1)
        if allowed is not None:
            score = jnp.where(jnp.concatenate([allowed] * H, axis=1), score, -1e30)
        scores.append(score)
    scores = jnp.concatenate(scores, axis=0)
    values = jnp.concatenate([values for _, values, _ in sources], axis=1)
    top = jnp.max(scores, axis=0, keepdims=True)
    expo = jnp.exp2((scores - top) * SCALE)
    total = jnp.sum(expo, axis=0, keepdims=True)
    weights = expo.astype(BF16)
    return top, total, [mm(values[head_rows(h)], weights[:, block(h)]) for h in range(H)]


def project(x, wk, wvt, k_held, v_held):
    k_held[...] = mm(x, wk).astype(BF16)
    values = mm_nt(wvt, x).astype(BF16)
    for s in range(x.shape[0] // BLK):
        v_held[s] = values[:, block(s)]


def named_slot(partner, s, link):
    row = lax.broadcasted_iota(jnp.int32, partner.shape, 0)
    column = lax.broadcasted_iota(jnp.int32, partner.shape, 1)
    return jnp.max(jnp.where((row == s) & (column == link), partner[...].astype(F32), 0.0)).astype(jnp.int32)


def far_source(slot, k_held, v_held):
    rows = pl.ds(pl.multiple_of(slot * BLK, BLK), BLK)
    return lambda p: k_held[rows, block(p)], v_held[slot], None


def own_kernel(partner, both, w, words, qs_out, wk_out, wvt_out, o_out, m_out, l_out, k_held, v_held):
    core = lax.axis_index("heads")
    wk_out[...] = w[1]
    wvt_out[...] = w[2].T
    q = mm(both[pl.ds(pl.multiple_of(core * ROWS, ROWS), ROWS)], w[0]).astype(BF16).T
    project(both[...], w[1], wvt_out[...], k_held, v_held)
    for s in range(SLOTS):
        for p in range(PAIRS):
            qs_out[s, p] = spread(q[block(p), block(s)])
        own_keys, own_values, _ = far_source(core * SLOTS + s, k_held, v_held)
        beside = far_source((1 - core) * SLOTS + named_slot(partner, s, 0), k_held, v_held)
        top, total, parts = attend(lambda p: qs_out[s, p], [(own_keys, own_values, local_mask(words[s])), beside])
        m_out[s] = top
        l_out[s] = total
        for h in range(H):
            o_out[head_rows(h), block(s)] = parts[h]


def pair_block(pair):
    return slice(2 * pair * BLK, 2 * (pair + 1) * BLK)


def merged(s, p, keys, values, qs, o_in, m_in, l_in):
    scores = mm(keys(p), qs[s, p])
    top = jnp.max(scores, axis=0, keepdims=True)
    m_old = m_in[s, :, pair_block(p)]
    m = jnp.maximum(m_old, top)
    old = jnp.exp2((m_old - m) * SCALE)
    expo = jnp.exp2((scores - m) * SCALE)
    l = l_in[s, :, pair_block(p)] * old + jnp.sum(expo, axis=0, keepdims=True)
    weights = expo.astype(BF16)
    o = [
        o_in[head_rows(2 * p + i), block(s)] * old[:, block(i)] + mm(values[head_rows(2 * p + i)], weights[:, block(i)])
        for i in range(2)
    ]
    return m, l, o


def far_kernel(link, partner, wk, wvt, qs, o_in, m_in, l_in, x, o_out, m_out, l_out, k_held, v_held):
    project(x[...], wk[...], wvt[...], k_held, v_held)
    slots = [named_slot(partner, s, link) for s in range(SLOTS)]
    for p in range(PAIRS):
        for s in range(SLOTS):
            keys, values, _ = far_source(slots[s], k_held, v_held)
            m, l, o = merged(s, p, keys, values, qs, o_in, m_in, l_in)
            m_out[s, :, pair_block(p)] = m
            l_out[s, :, pair_block(p)] = l
            for i in range(2):
                o_out[head_rows(2 * p + i), block(s)] = o[i]


def last_kernel(
    link, partner, counts, wk, wvt, qs, o_in, m_in, l_in, both_x, w_out, w_up, w_down, r, out, k_held, v_held, att, done, sems,
):
    core = lax.axis_index("heads")
    project(r[pl.ds(0, ROWS)], wk[...], wvt[...], k_held, v_held)
    slots = [named_slot(partner, s, link) for s in range(SLOTS)]
    for p in range(PAIRS):
        for s in range(SLOTS):
            keys, values, _ = far_source(slots[s], k_held, v_held)
            _, l, o = merged(s, p, keys, values, qs, o_in, m_in, l_in)
            share = 1.0 / l
            o = jnp.concatenate([o[i] * share[:, block(i)] for i in range(2)], axis=0)
            att[block(s), block(p)] = o.astype(BF16).T
    x = both_x[pl.ds(pl.multiple_of(core * ROWS, ROWS), ROWS)]
    resid = x.astype(F32) + mm(att[...], w_out[...])
    mean = jnp.mean(resid, axis=1, keepdims=True)
    var = jnp.mean(resid * resid, axis=1, keepdims=True) - mean * mean
    normed = (resid - mean) * lax.rsqrt(var + EPSILON)
    hidden = jnp.maximum(mm(normed.astype(BF16), w_up[...]).astype(BF16), 0.0)
    copies = []
    for i, rows in enumerate((slice(0, 2 * BLK), slice(2 * BLK, ROWS))):
        mixed = normed[rows] + mm(hidden[rows], w_down[...])
        slot = lax.broadcasted_iota(jnp.int32, (mixed.shape[0], 1), 0) // BLK + 2 * i
        done[rows] = jnp.where(slot < counts[...], mixed, 0.0).astype(BF16)
        copies.append(pltpu.make_async_copy(done.at[rows], out.at[rows], sems.at[i]))
        copies[i].start()
    for copy in copies:
        copy.wait()


VMEM = pl.BlockSpec(memory_space=pltpu.VMEM)
SPREAD = jax.ShapeDtypeStruct((SLOTS, PAIRS, BLK, 2 * BLK), BF16)
WEIGHT = jax.ShapeDtypeStruct((D, D), BF16)
STATE = (
    jax.ShapeDtypeStruct((D, ROWS), F32),
    jax.ShapeDtypeStruct((SLOTS, 1, H * BLK), F32),
    jax.ShapeDtypeStruct((SLOTS, 1, H * BLK), F32),
)
HELD = [pltpu.VMEM((ROWS, D), BF16), pltpu.VMEM((SLOTS, D, BLK), BF16)]
BOTH_HELD = [pltpu.VMEM((2 * ROWS, D), BF16), pltpu.VMEM((2 * SLOTS, D, BLK), BF16)]


PAD = ROWS + 16


def stage_kernel(x, x_out, sems):
    copies = [
        pltpu.make_async_copy(x, x_out.at[pl.ds(0, ROWS)], sems.at[0]),
        pltpu.make_async_copy(x.at[pl.ds(0, PAD - ROWS)], x_out.at[pl.ds(ROWS, PAD - ROWS)], sems.at[1]),
    ]
    for copy in copies:
        copy.start()
    for copy in copies:
        copy.wait()


def stage(x):
    return pl.pallas_call(
        stage_kernel,
        out_shape=jax.ShapeDtypeStruct((PAD, D), BF16),
        in_specs=[pl.BlockSpec(memory_space=pltpu.HBM)],
        out_specs=VMEM,
        scratch_shapes=[pltpu.SemaphoreType.DMA((2,))],
        compiler_params=pltpu.CompilerParams(vmem_limit_bytes=4 * 2**20),
        cost_estimate=pl.CostEstimate(flops=0, bytes_accessed=0, transcendentals=0),
        name="stage",
    )(x)


def call(kernel, scalars, inside, outs, scratch, name, out_space=pltpu.VMEM):
    return pl.pallas_call(
        kernel,
        out_shape=outs,
        in_specs=[VMEM] * (len(scalars) + len(inside)),
        out_specs=jax.tree.map(lambda _: pl.BlockSpec(memory_space=out_space), outs),
        scratch_shapes=scratch,
        compiler_params=pltpu.CompilerParams(vmem_limit_bytes=12 * 2**20),
        cost_estimate=pl.CostEstimate(flops=0, bytes_accessed=0, transcendentals=0),
        name=name,
    )(*scalars, *inside)


def local(features, w_qkv, w_out, w_up, w_down, pattern, partner, counts):
    log_size = (lax.axis_size("nodes") * lax.axis_size("heads")).bit_length() - 1
    bits = [link * log_size // 4 for link in range(4)]

    def exchange(value, link):
        return from_partner(value, "nodes", bits[link] - 1)

    w = jnp.transpose(w_qkv, (1, 0, 2))
    words = jnp.transpose(pattern, (0, 2, 1))
    received = {2: exchange(stage(features), 2)}
    for link in (1, 3):
        received[link] = exchange(features, link)
    both = lax.all_gather(features, "heads").reshape(2 * ROWS, D)
    qs, wk, wvt, *state = call(
        own_kernel, [partner], [both, w, words], (SPREAD, WEIGHT, WEIGHT, *STATE), BOTH_HELD, "own"
    )
    fixed = (wk, wvt, qs)
    for link in (1, 3):
        state = call(
            lambda *refs, link=link: far_kernel(link, *refs), [partner], [*fixed, *state, received[link]], STATE, HELD, "far"
        )
    return call(
        lambda *refs: last_kernel(2, *refs), [partner, counts.reshape(1, 1)],
        [*fixed, *state, both, w_out, w_up, w_down, received[2]],
        jax.ShapeDtypeStruct((ROWS, D), BF16),
        [*HELD, *[pltpu.VMEM((ROWS, D), BF16)] * 2, pltpu.SemaphoreType.DMA((SLOTS,))], "last", pltpu.HBM,
    )


def solution(mesh):
    placed = (
        P(("nodes", "heads"), None),
        P(),
        P(),
        P(),
        P(),
        P(("nodes", "heads"), None, None),
        P(("nodes", "heads"), None),
        P(("nodes", "heads")),
    )
    return jax.shard_map(
        local, mesh=mesh, in_specs=placed, out_specs=P(("nodes", "heads"), None), check_vma=False
    )
```

```python
import jax
import jax.numpy as jnp
from jax import lax
from jax.experimental import pallas as pl
from jax.experimental.pallas import tpu as pltpu
from jax.sharding import PartitionSpec as P

D = 512
H = 8
HEAD = D // H
BLK = 128
SLOTS = 3
ROWS = SLOTS * BLK
PAIRS = H // 2
EPSILON = 1e-05
SCALE = 1.4426950408889634 / HEAD**0.5
F32 = jnp.float32
BF16 = jnp.bfloat16


def from_partner(value, axis, bit):
    mask = 2**bit
    pairs = [(source, source ^ mask) for source in range(lax.axis_size(axis))]
    return lax.ppermute(value, axis, pairs)


def mm(a, b):
    return jnp.dot(a, b, preferred_element_type=F32)


def mm_nt(a, b):
    return lax.dot_general(a, b, (((1,), (1,)), ((), ())), preferred_element_type=F32)


def block(index):
    return slice(index * BLK, (index + 1) * BLK)


def head_rows(head):
    return slice(head * HEAD, (head + 1) * HEAD)


def local_mask(words):
    word_count = words.shape[0]
    halves = jnp.concatenate([words & 255, jnp.right_shift(words, 8)], axis=0).astype(F32).astype(BF16)
    key = lax.broadcasted_iota(jnp.int32, (BLK, 2 * word_count), 0)
    row = lax.broadcasted_iota(jnp.int32, (BLK, 2 * word_count), 1)
    source = key // 16 + word_count * (key % 16 // 8)
    pick = jnp.where(row == source, 1.0, 0.0).astype(BF16)
    picked = mm(pick, halves)
    key = lax.broadcasted_iota(jnp.int32, (BLK, BLK), 0)
    query = lax.broadcasted_iota(jnp.int32, (BLK, BLK), 1)
    bits = jnp.right_shift(picked.astype(jnp.int32), key % 8) & 1
    return (bits == 1) | (query == key)


def spread(q_pair):
    low = lax.broadcasted_iota(jnp.int32, q_pair.shape, 0) < HEAD
    zero = jnp.zeros_like(q_pair)
    return jnp.concatenate([jnp.where(low, q_pair, zero), jnp.where(low, zero, q_pair)], axis=1)


def attend(q_spread, sources):
    scores = []
    for keys, _, allowed in sources:
        score = jnp.concatenate([mm(keys(p), q_spread(p)) for p in range(PAIRS)], axis=1)
        if allowed is not None:
            score = jnp.where(jnp.concatenate([allowed] * H, axis=1), score, -1e30)
        scores.append(score)
    scores = jnp.concatenate(scores, axis=0)
    values = jnp.concatenate([values for _, values, _ in sources], axis=1)
    top = jnp.max(scores, axis=0, keepdims=True)
    expo = jnp.exp2((scores - top) * SCALE)
    total = jnp.sum(expo, axis=0, keepdims=True)
    weights = expo.astype(BF16)
    return top, total, [mm(values[head_rows(h)], weights[:, block(h)]) for h in range(H)]


def project(x, wk, wvt, k_held, v_held):
    k_held[...] = mm(x, wk).astype(BF16)
    values = mm_nt(wvt, x).astype(BF16)
    for s in range(x.shape[0] // BLK):
        v_held[s] = values[:, block(s)]


def named_slot(partner, s, link):
    row = lax.broadcasted_iota(jnp.int32, partner.shape, 0)
    column = lax.broadcasted_iota(jnp.int32, partner.shape, 1)
    return jnp.max(jnp.where((row == s) & (column == link), partner[...].astype(F32), 0.0)).astype(jnp.int32)


def far_source(slot, k_held, v_held):
    rows = pl.ds(pl.multiple_of(slot * BLK, BLK), BLK)
    return lambda p: k_held[rows, block(p)], v_held[slot], None


def own_kernel(partner, both, w, words, qs_out, wk_out, wvt_out, o_out, m_out, l_out, k_held, v_held):
    core = lax.axis_index("heads")
    wk_out[...] = w[1]
    wvt_out[...] = w[2].T
    q = mm(both[pl.ds(pl.multiple_of(core * ROWS, ROWS), ROWS)], w[0]).astype(BF16).T
    project(both[...], w[1], wvt_out[...], k_held, v_held)
    for s in range(SLOTS):
        for p in range(PAIRS):
            qs_out[s, p] = spread(q[block(p), block(s)])
        own_keys, own_values, _ = far_source(core * SLOTS + s, k_held, v_held)
        beside = far_source((1 - core) * SLOTS + named_slot(partner, s, 0), k_held, v_held)
        top, total, parts = attend(lambda p: qs_out[s, p], [(own_keys, own_values, local_mask(words[s])), beside])
        m_out[s] = top
        l_out[s] = total
        for h in range(H):
            o_out[head_rows(h), block(s)] = parts[h]


def pair_block(pair):
    return slice(2 * pair * BLK, 2 * (pair + 1) * BLK)


def merged(s, p, keys, values, qs, o_in, m_in, l_in):
    scores = mm(keys(p), qs[s, p])
    top = jnp.max(scores, axis=0, keepdims=True)
    m_old = m_in[s, :, pair_block(p)]
    m = jnp.maximum(m_old, top)
    old = jnp.exp2((m_old - m) * SCALE)
    expo = jnp.exp2((scores - m) * SCALE)
    l = l_in[s, :, pair_block(p)] * old + jnp.sum(expo, axis=0, keepdims=True)
    weights = expo.astype(BF16)
    o = [
        o_in[head_rows(2 * p + i), block(s)] * old[:, block(i)] + mm(values[head_rows(2 * p + i)], weights[:, block(i)])
        for i in range(2)
    ]
    return m, l, o


def far_kernel(link, partner, wk, wvt, qs, o_in, m_in, l_in, x, o_out, m_out, l_out, k_held, v_held):
    project(x[...], wk[...], wvt[...], k_held, v_held)
    slots = [named_slot(partner, s, link) for s in range(SLOTS)]
    for p in range(PAIRS):
        for s in range(SLOTS):
            keys, values, _ = far_source(slots[s], k_held, v_held)
            m, l, o = merged(s, p, keys, values, qs, o_in, m_in, l_in)
            m_out[s, :, pair_block(p)] = m
            l_out[s, :, pair_block(p)] = l
            for i in range(2):
                o_out[head_rows(2 * p + i), block(s)] = o[i]


def last_kernel(
    link, partner, counts, wk, wvt, qs, o_in, m_in, l_in, both_x, w_out, w_up, w_down, r, out, k_held, v_held, att, done, sems,
):
    core = lax.axis_index("heads")
    project(r[pl.ds(0, ROWS)], wk[...], wvt[...], k_held, v_held)
    slots = [named_slot(partner, s, link) for s in range(SLOTS)]
    for p in range(PAIRS):
        for s in range(SLOTS):
            keys, values, _ = far_source(slots[s], k_held, v_held)
            _, l, o = merged(s, p, keys, values, qs, o_in, m_in, l_in)
            share = 1.0 / l
            o = jnp.concatenate([o[i] * share[:, block(i)] for i in range(2)], axis=0)
            att[block(s), block(p)] = o.astype(BF16).T
    x = both_x[pl.ds(pl.multiple_of(core * ROWS, ROWS), ROWS)]
    resid = x.astype(F32) + mm(att[...], w_out[...])
    mean = jnp.mean(resid, axis=1, keepdims=True)
    var = jnp.mean(resid * resid, axis=1, keepdims=True) - mean * mean
    normed = (resid - mean) * lax.rsqrt(var + EPSILON)
    hidden = jnp.maximum(mm(normed.astype(BF16), w_up[...]).astype(BF16), 0.0)
    copies = []
    for i, rows in enumerate((slice(0, 2 * BLK), slice(2 * BLK, ROWS))):
        mixed = normed[rows] + mm(hidden[rows], w_down[...])
        slot = lax.broadcasted_iota(jnp.int32, (mixed.shape[0], 1), 0) // BLK + 2 * i
        done[rows] = jnp.where(slot < counts[...], mixed, 0.0).astype(BF16)
        copies.append(pltpu.make_async_copy(done.at[rows], out.at[rows], sems.at[i]))
        copies[i].start()
    for copy in copies:
        copy.wait()


VMEM = pl.BlockSpec(memory_space=pltpu.VMEM)
SPREAD = jax.ShapeDtypeStruct((SLOTS, PAIRS, BLK, 2 * BLK), BF16)
WEIGHT = jax.ShapeDtypeStruct((D, D), BF16)
STATE = (
    jax.ShapeDtypeStruct((D, ROWS), F32),
    jax.ShapeDtypeStruct((SLOTS, 1, H * BLK), F32),
    jax.ShapeDtypeStruct((SLOTS, 1, H * BLK), F32),
)
HELD = [pltpu.VMEM((ROWS, D), BF16), pltpu.VMEM((SLOTS, D, BLK), BF16)]
BOTH_HELD = [pltpu.VMEM((2 * ROWS, D), BF16), pltpu.VMEM((2 * SLOTS, D, BLK), BF16)]


PAD = ROWS + 8


def stage_kernel(x, x_out, sem):
    copy = pltpu.make_async_copy(x, x_out.at[pl.ds(0, ROWS)], sem)
    copy.start()
    copy.wait()


def stage(x):
    return pl.pallas_call(
        stage_kernel,
        out_shape=jax.ShapeDtypeStruct((PAD, D), BF16),
        in_specs=[pl.BlockSpec(memory_space=pltpu.HBM)],
        out_specs=VMEM,
        scratch_shapes=[pltpu.SemaphoreType.DMA],
        compiler_params=pltpu.CompilerParams(vmem_limit_bytes=4 * 2**20),
        cost_estimate=pl.CostEstimate(flops=0, bytes_accessed=0, transcendentals=0),
        name="stage",
    )(x)


def call(kernel, scalars, inside, outs, scratch, name, out_space=pltpu.VMEM):
    return pl.pallas_call(
        kernel,
        out_shape=outs,
        in_specs=[VMEM] * (len(scalars) + len(inside)),
        out_specs=jax.tree.map(lambda _: pl.BlockSpec(memory_space=out_space), outs),
        scratch_shapes=scratch,
        compiler_params=pltpu.CompilerParams(vmem_limit_bytes=12 * 2**20),
        cost_estimate=pl.CostEstimate(flops=0, bytes_accessed=0, transcendentals=0),
        name=name,
    )(*scalars, *inside)


def local(features, w_qkv, w_out, w_up, w_down, pattern, partner, counts):
    log_size = (lax.axis_size("nodes") * lax.axis_size("heads")).bit_length() - 1
    bits = [link * log_size // 4 for link in range(4)]

    def exchange(value, link):
        return from_partner(value, "nodes", bits[link] - 1)

    w = jnp.transpose(w_qkv, (1, 0, 2))
    words = jnp.transpose(pattern, (0, 2, 1))
    received = {2: exchange(stage(features), 2)}
    for link in (1, 3):
        received[link] = exchange(features, link)
    both = lax.all_gather(features, "heads").reshape(2 * ROWS, D)
    qs, wk, wvt, *state = call(
        own_kernel, [partner], [both, w, words], (SPREAD, WEIGHT, WEIGHT, *STATE), BOTH_HELD, "own"
    )
    fixed = (wk, wvt, qs)
    for link in (1, 3):
        state = call(
            lambda *refs, link=link: far_kernel(link, *refs), [partner], [*fixed, *state, received[link]], STATE, HELD, "far"
        )
    return call(
        lambda *refs: last_kernel(2, *refs), [partner, counts.reshape(1, 1)],
        [*fixed, *state, both, w_out, w_up, w_down, received[2]],
        jax.ShapeDtypeStruct((ROWS, D), BF16),
        [*HELD, *[pltpu.VMEM((ROWS, D), BF16)] * 2, pltpu.SemaphoreType.DMA((SLOTS,))], "last", pltpu.HBM,
    )


def solution(mesh):
    placed = (
        P(("nodes", "heads"), None),
        P(),
        P(),
        P(),
        P(),
        P(("nodes", "heads"), None, None),
        P(("nodes", "heads"), None),
        P(("nodes", "heads")),
    )
    return jax.shard_map(
        local, mesh=mesh, in_specs=placed, out_specs=P(("nodes", "heads"), None), check_vma=False
    )
```

```python
import jax
import jax.numpy as jnp
from jax import lax
from jax.experimental import pallas as pl
from jax.experimental.pallas import tpu as pltpu
from jax.sharding import PartitionSpec as P

D = 512
H = 8
HEAD = D // H
BLK = 128
SLOTS = 3
ROWS = SLOTS * BLK
PAIRS = H // 2
EPSILON = 1e-05
SCALE = 1.4426950408889634 / HEAD**0.5
F32 = jnp.float32
BF16 = jnp.bfloat16


def from_partner(value, axis, bit):
    mask = 2**bit
    pairs = [(source, source ^ mask) for source in range(lax.axis_size(axis))]
    return lax.ppermute(value, axis, pairs)


def mm(a, b):
    return jnp.dot(a, b, preferred_element_type=F32)


def mm_nt(a, b):
    return lax.dot_general(a, b, (((1,), (1,)), ((), ())), preferred_element_type=F32)


def block(index):
    return slice(index * BLK, (index + 1) * BLK)


def head_rows(head):
    return slice(head * HEAD, (head + 1) * HEAD)


def local_mask(words):
    word_count = words.shape[0]
    halves = jnp.concatenate([words & 255, jnp.right_shift(words, 8)], axis=0).astype(F32).astype(BF16)
    key = lax.broadcasted_iota(jnp.int32, (BLK, 2 * word_count), 0)
    row = lax.broadcasted_iota(jnp.int32, (BLK, 2 * word_count), 1)
    source = key // 16 + word_count * (key % 16 // 8)
    pick = jnp.where(row == source, 1.0, 0.0).astype(BF16)
    picked = mm(pick, halves)
    key = lax.broadcasted_iota(jnp.int32, (BLK, BLK), 0)
    query = lax.broadcasted_iota(jnp.int32, (BLK, BLK), 1)
    bits = jnp.right_shift(picked.astype(jnp.int32), key % 8) & 1
    return (bits == 1) | (query == key)


def spread(q_pair):
    low = lax.broadcasted_iota(jnp.int32, q_pair.shape, 0) < HEAD
    zero = jnp.zeros_like(q_pair)
    return jnp.concatenate([jnp.where(low, q_pair, zero), jnp.where(low, zero, q_pair)], axis=1)


def attend(q_spread, sources):
    scores = []
    for keys, _, allowed in sources:
        score = jnp.concatenate([mm(keys(p), q_spread(p)) for p in range(PAIRS)], axis=1)
        if allowed is not None:
            score = jnp.where(jnp.concatenate([allowed] * H, axis=1), score, -1e30)
        scores.append(score)
    scores = jnp.concatenate(scores, axis=0)
    values = jnp.concatenate([values for _, values, _ in sources], axis=1)
    top = jnp.max(scores, axis=0, keepdims=True)
    expo = jnp.exp2((scores - top) * SCALE)
    total = jnp.sum(expo, axis=0, keepdims=True)
    weights = expo.astype(BF16)
    return top, total, [mm(values[head_rows(h)], weights[:, block(h)]) for h in range(H)]


def project(x, wk, wvt, k_held, v_held):
    k_held[...] = mm(x, wk).astype(BF16)
    values = mm_nt(wvt, x).astype(BF16)
    for s in range(x.shape[0] // BLK):
        v_held[s] = values[:, block(s)]


def named_slot(partner, s, link):
    row = lax.broadcasted_iota(jnp.int32, partner.shape, 0)
    column = lax.broadcasted_iota(jnp.int32, partner.shape, 1)
    return jnp.max(jnp.where((row == s) & (column == link), partner[...].astype(F32), 0.0)).astype(jnp.int32)


def far_source(slot, k_held, v_held):
    rows = pl.ds(pl.multiple_of(slot * BLK, BLK), BLK)
    return lambda p: k_held[rows, block(p)], v_held[slot], None


def own_kernel(partner, both, w, words, qs_out, wvt_out, o_out, m_out, l_out, k_held, v_held):
    core = lax.axis_index("heads")
    wvt_out[...] = w[2].T
    q = mm(both[pl.ds(pl.multiple_of(core * ROWS, ROWS), ROWS)], w[0]).astype(BF16).T
    project(both[...], w[1], wvt_out[...], k_held, v_held)
    for s in range(SLOTS):
        for p in range(PAIRS):
            qs_out[s, p] = spread(q[block(p), block(s)])
        own_keys, own_values, _ = far_source(core * SLOTS + s, k_held, v_held)
        beside = far_source((1 - core) * SLOTS + named_slot(partner, s, 0), k_held, v_held)
        top, total, parts = attend(lambda p: qs_out[s, p], [(own_keys, own_values, local_mask(words[s])), beside])
        m_out[s] = top
        l_out[s] = total
        for h in range(H):
            o_out[head_rows(h), block(s)] = parts[h]


def pair_block(pair):
    return slice(2 * pair * BLK, 2 * (pair + 1) * BLK)


def merged(s, p, keys, values, qs, o_in, m_in, l_in):
    scores = mm(keys(p), qs[s, p])
    top = jnp.max(scores, axis=0, keepdims=True)
    m_old = m_in[s, :, pair_block(p)]
    m = jnp.maximum(m_old, top)
    old = jnp.exp2((m_old - m) * SCALE)
    expo = jnp.exp2((scores - m) * SCALE)
    l = l_in[s, :, pair_block(p)] * old + jnp.sum(expo, axis=0, keepdims=True)
    weights = expo.astype(BF16)
    o = [
        o_in[head_rows(2 * p + i), block(s)] * old[:, block(i)] + mm(values[head_rows(2 * p + i)], weights[:, block(i)])
        for i in range(2)
    ]
    return m, l, o


def far_kernel(link, partner, w, wvt, qs, o_in, m_in, l_in, x, o_out, m_out, l_out, k_held, v_held):
    project(x[...], w[1], wvt[...], k_held, v_held)
    slots = [named_slot(partner, s, link) for s in range(SLOTS)]
    for p in range(PAIRS):
        for s in range(SLOTS):
            keys, values, _ = far_source(slots[s], k_held, v_held)
            m, l, o = merged(s, p, keys, values, qs, o_in, m_in, l_in)
            m_out[s, :, pair_block(p)] = m
            l_out[s, :, pair_block(p)] = l
            for i in range(2):
                o_out[head_rows(2 * p + i), block(s)] = o[i]


def last_kernel(
    link, partner, counts, w, wvt, qs, o_in, m_in, l_in, both_x, w_out, w_up, w_down, r, out, k_held, v_held, att, done, sems,
):
    core = lax.axis_index("heads")
    project(r[pl.ds(0, ROWS)], w[1], wvt[...], k_held, v_held)
    slots = [named_slot(partner, s, link) for s in range(SLOTS)]
    for p in range(PAIRS):
        for s in range(SLOTS):
            keys, values, _ = far_source(slots[s], k_held, v_held)
            _, l, o = merged(s, p, keys, values, qs, o_in, m_in, l_in)
            share = 1.0 / l
            o = jnp.concatenate([o[i] * share[:, block(i)] for i in range(2)], axis=0)
            att[block(s), block(p)] = o.astype(BF16).T
    x = both_x[pl.ds(pl.multiple_of(core * ROWS, ROWS), ROWS)]
    resid = x.astype(F32) + mm(att[...], w_out[...])
    mean = jnp.mean(resid, axis=1, keepdims=True)
    var = jnp.mean(resid * resid, axis=1, keepdims=True) - mean * mean
    normed = (resid - mean) * lax.rsqrt(var + EPSILON)
    hidden = jnp.maximum(mm(normed.astype(BF16), w_up[...]).astype(BF16), 0.0)
    copies = []
    for i, rows in enumerate((slice(0, 2 * BLK), slice(2 * BLK, ROWS))):
        mixed = normed[rows] + mm(hidden[rows], w_down[...])
        slot = lax.broadcasted_iota(jnp.int32, (mixed.shape[0], 1), 0) // BLK + 2 * i
        done[rows] = jnp.where(slot < counts[...], mixed, 0.0).astype(BF16)
        copies.append(pltpu.make_async_copy(done.at[rows], out.at[rows], sems.at[i]))
        copies[i].start()
    for copy in copies:
        copy.wait()


VMEM = pl.BlockSpec(memory_space=pltpu.VMEM)
SPREAD = jax.ShapeDtypeStruct((SLOTS, PAIRS, BLK, 2 * BLK), BF16)
WEIGHT = jax.ShapeDtypeStruct((D, D), BF16)
STATE = (
    jax.ShapeDtypeStruct((D, ROWS), F32),
    jax.ShapeDtypeStruct((SLOTS, 1, H * BLK), F32),
    jax.ShapeDtypeStruct((SLOTS, 1, H * BLK), F32),
)
HELD = [pltpu.VMEM((ROWS, D), BF16), pltpu.VMEM((SLOTS, D, BLK), BF16)]
BOTH_HELD = [pltpu.VMEM((2 * ROWS, D), BF16), pltpu.VMEM((2 * SLOTS, D, BLK), BF16)]


PAD = ROWS + 8


def stage_kernel(x, x_out, sem):
    copy = pltpu.make_async_copy(x, x_out.at[pl.ds(0, ROWS)], sem)
    copy.start()
    copy.wait()


def stage(x):
    return pl.pallas_call(
        stage_kernel,
        out_shape=jax.ShapeDtypeStruct((PAD, D), BF16),
        in_specs=[pl.BlockSpec(memory_space=pltpu.HBM)],
        out_specs=VMEM,
        scratch_shapes=[pltpu.SemaphoreType.DMA],
        compiler_params=pltpu.CompilerParams(vmem_limit_bytes=4 * 2**20),
        cost_estimate=pl.CostEstimate(flops=0, bytes_accessed=0, transcendentals=0),
        name="stage",
    )(x)


def call(kernel, scalars, inside, outs, scratch, name, out_space=pltpu.VMEM):
    return pl.pallas_call(
        kernel,
        out_shape=outs,
        in_specs=[VMEM] * (len(scalars) + len(inside)),
        out_specs=jax.tree.map(lambda _: pl.BlockSpec(memory_space=out_space), outs),
        scratch_shapes=scratch,
        compiler_params=pltpu.CompilerParams(vmem_limit_bytes=12 * 2**20),
        cost_estimate=pl.CostEstimate(flops=0, bytes_accessed=0, transcendentals=0),
        name=name,
    )(*scalars, *inside)


def local(features, w_qkv, w_out, w_up, w_down, pattern, partner, counts):
    log_size = (lax.axis_size("nodes") * lax.axis_size("heads")).bit_length() - 1
    bits = [link * log_size // 4 for link in range(4)]

    def exchange(value, link):
        return from_partner(value, "nodes", bits[link] - 1)

    w = jnp.transpose(w_qkv, (1, 0, 2))
    words = jnp.transpose(pattern, (0, 2, 1))
    received = {2: exchange(stage(features), 2)}
    for link in (1, 3):
        received[link] = exchange(features, link)
    both = lax.all_gather(features, "heads").reshape(2 * ROWS, D)
    qs, wvt, *state = call(
        own_kernel, [partner], [both, w, words], (SPREAD, WEIGHT, *STATE), BOTH_HELD, "own"
    )
    fixed = (w, wvt, qs)
    for link in (1, 3):
        state = call(
            lambda *refs, link=link: far_kernel(link, *refs), [partner], [*fixed, *state, received[link]], STATE, HELD, "far"
        )
    return call(
        lambda *refs: last_kernel(2, *refs), [partner, counts.reshape(1, 1)],
        [*fixed, *state, both, w_out, w_up, w_down, received[2]],
        jax.ShapeDtypeStruct((ROWS, D), BF16),
        [*HELD, *[pltpu.VMEM((ROWS, D), BF16)] * 2, pltpu.SemaphoreType.DMA((SLOTS,))], "last", pltpu.HBM,
    )


def solution(mesh):
    placed = (
        P(("nodes", "heads"), None),
        P(),
        P(),
        P(),
        P(),
        P(("nodes", "heads"), None, None),
        P(("nodes", "heads"), None),
        P(("nodes", "heads")),
    )
    return jax.shard_map(
        local, mesh=mesh, in_specs=placed, out_specs=P(("nodes", "heads"), None), check_vma=False
    )
```
